512 devices in a mesh: lon: 16 (over y, z_hi, core), frame: 32 (over x, z_lo).
Axes of the slice: x: 4, y: 4, z: 16 (z_hi: 2, z_lo: 8; z = z_hi * 8 + z_lo), core: 2. Of those that a mesh axis runs over, the one named last changes fastest.
Arguments:
- latents: bfloat16 [160, 32, 64, 640], P('frame', None, 'lon'), may hold values from -6 to 6
- spatial_kernel: bfloat16 [5760, 640], P('frame', 'lon'), may hold values from -0.078125 to 0.078125
- spatial_bias: float32 [640], replicated, may hold values from -4 to 4
- temporal_kernel: bfloat16 [1920, 640], replicated, may hold values from -0.125 to 0.125
- temporal_bias: float32 [640], replicated, may hold values from -4 to 4
Outputs:
- block_output: bfloat16 [160, 32, 64, 640], P('frame', None, 'lon')
The draws below stay inside these ranges and needn't reach their ends.
All inputs are finite; a program needn't handle non-finite values.
Results may differ from the reference program's by a relative error of at most 0.0031.
Values may be sent and summed in bfloat16 or wider, within the bound.
No kernel may reach another device: no remote copies, remote signals or barrier semaphores. Data moves between devices by JAX's collectives and lax.ppermute only.
A program may use at most 128 MiB of HBM per device.

```python
import jax
import jax.numpy as jnp
from jax import lax

C = 640
LAT = 32
FRAMES = 160
LON = 64


def level_of(own_key, shape, pieces, low, top_value):
    gain = 1.0
    for position, shards_of in pieces:
        heights = jax.random.uniform(jax.random.fold_in(jax.random.fold_in(own_key, 6), position), (shards_of,), jnp.float32, low / len(pieces), top_value / len(pieces))
        gain = gain * jnp.repeat(jnp.exp(heights), shape[position] // shards_of).reshape((-1,) + (1,) * (len(shape) - 1 - position))
    return gain


def normal_values(key, shape, scale, bound, shards=(), dtype=jnp.bfloat16):
    loudness = level_of(key, shape, shards, -0.22, 0.18) if shards else 1.0
    drawn = jax.random.normal(key, shape, jnp.float32) * scale * loudness
    return jnp.minimum(jnp.maximum(drawn, -bound), bound).astype(dtype)


def setup_inputs(seed: int = 0) -> dict:
    key_list = jax.random.split(jax.random.key(seed), 6)
    return {
        "latents": normal_values(key_list[0], (FRAMES, LAT, LON, C), 1.0, 6.0, ((0, 32), (2, 16))),
        "spatial_kernel": normal_values(key_list[1], (9 * C, C), (9 * C) ** -0.5, 0.078125, ((0, 32), (1, 16))),
        "spatial_bias": normal_values(key_list[2], (C,), 1.0, 4.0, (), jnp.float32),
        "temporal_kernel": normal_values(key_list[3], (3 * C, C), (3 * C) ** -0.5, 0.125),
        "temporal_bias": normal_values(key_list[4], (C,), 1.0, 4.0, (), jnp.float32),
    }


def collect_taps(padded, lat_rows, lon_cols):
    columns = []
    for offset_lat in range(3):
        for offset_lon in range(3):
            columns.append(padded[..., offset_lat:offset_lat + lat_rows, offset_lon:offset_lon + lon_cols, :])
    return jnp.concatenate(columns, axis=-1)


def reference(latents, spatial_kernel, spatial_bias, temporal_kernel, temporal_bias):
    channels = latents.shape[-1]
    wrapped = jnp.concatenate([latents[:, :, -1:], latents, latents[:, :, :1]], axis=2)
    padded = jnp.pad(wrapped, ((0, 0), (1, 1), (0, 0), (0, 0)))

    def spatial_frame(frame_block):
        tap_rows = collect_taps(frame_block, LAT, LON).reshape(LAT * LON, 9 * channels)
        summed = jnp.dot(tap_rows, spatial_kernel, preferred_element_type=jnp.float32) + spatial_bias
        return jax.nn.silu(summed).astype(jnp.bfloat16).reshape(LAT, LON, channels)

    hidden = lax.map(spatial_frame, padded)
    framed = jnp.pad(hidden, ((1, 1), (0, 0), (0, 0), (0, 0)))

    def temporal_frame(inputs):
        before, middle, later_frame, source = inputs
        stacked = jnp.concatenate([before, middle, later_frame], axis=-1).reshape(LAT * LON, 3 * channels)
        mixed = jnp.dot(stacked, temporal_kernel, preferred_element_type=jnp.float32) + temporal_bias
        return (source.astype(jnp.float32) + jax.nn.silu(mixed).reshape(LAT, LON, channels)).astype(jnp.bfloat16)

    return lax.map(temporal_frame, (framed[:-2], framed[1:-1], framed[2:], latents))
```

```python
import jax
import jax.numpy as jnp
from jax import lax
from jax.sharding import PartitionSpec as P

LONS = 16
FRAMES_AXIS = 32
Y = 4
X = 4
Z_LO = 8


def lon_index(y, z_hi, core):
    return y * 4 + z_hi * 2 + core


def frame_index(x, z_lo):
    return x * Z_LO + z_lo


def z_groups():
    return [
        [
            lon_index(y, z_hi, core) * FRAMES_AXIS + frame_index(x, z_lo)
            for z_hi in range(2)
            for z_lo in range(Z_LO)
        ]
        for x in range(X)
        for y in range(Y)
        for core in range(2)
    ]


def x_groups():
    return [[frame_index(x, z_lo) for x in range(X)] for z_lo in range(Z_LO)]


def from_y(k):
    return [(((y + k) % Y) * 4 + r, y * 4 + r) for y in range(Y) for r in range(4)]


CORES = [(i, i ^ 1) for i in range(LONS)]
FAR = [(i, (i + 1) % LONS if i % 2 else (i - 1) % LONS) for i in range(LONS)]


def copies(piece, count):
    return jnp.broadcast_to(piece[None], (count,) + piece.shape)


def gather_rows(spatial_kernel):
    shard = spatial_kernel.T
    cols, rows = shard.shape
    along_z = lax.all_to_all(
        copies(shard, 16), ("lon", "frame"), 0, 0, axis_index_groups=z_groups()
    )
    along_z = along_z.reshape(2, Z_LO, cols, rows).transpose(0, 2, 1, 3)
    along_z = along_z.reshape(2 * cols, Z_LO * rows)
    along_x = lax.all_to_all(copies(along_z, X), "frame", 0, 0, axis_index_groups=x_groups())
    return along_x.transpose(1, 0, 2).reshape(2 * cols, X * Z_LO * rows)


def own_order(blocks, axis):
    lon = lax.axis_index("lon")
    y, core = lon // 4, lon % 2
    shape = blocks.shape
    split = blocks.reshape(shape[:axis] + (Y, 2, 2, 40) + shape[axis + 1 :])
    twice = jnp.concatenate([split, split], axis=axis)
    turned = lax.dynamic_slice_in_dim(twice, y, Y, axis=axis)
    first = jnp.take(turned, jnp.array(0), axis=axis + 2)
    second = jnp.take(turned, jnp.array(1), axis=axis + 2)
    own = jnp.where(core == 0, first, second)
    other = jnp.where(core == 0, second, first)
    return jnp.concatenate([own, other], axis=axis).reshape(shape)


def body(latents, spatial_kernel, spatial_bias, temporal_kernel, temporal_bias):
    frames, lat_rows, lon_cols, channels = latents.shape
    positions = frames * lat_rows
    core = lax.axis_index("lon") % 2
    mine = gather_rows(spatial_kernel)

    mine, latents_then = lax.optimization_barrier((mine, latents))
    pieces = [mine] + [lax.ppermute(mine, "lon", from_y(k)) for k in (1, 2, 3)]
    columns = latents_then.transpose(2, 0, 1, 3)
    far = lax.ppermute(jnp.where(core == 1, columns[-1], columns[0]), "lon", FAR)
    near = lax.ppermute(jnp.where(core == 1, columns[0], columns[-1]), "lon", CORES)
    before = jnp.where(core == 1, near, far)
    after = jnp.where(core == 1, far, near)
    wide = jnp.concatenate([before[None], columns, after[None]], axis=0)
    wide = jnp.pad(wide, ((0, 0), (0, 0), (1, 1), (0, 0)))
    taps = [
        wide[b : b + lon_cols, :, a : a + lat_rows].reshape(lon_cols * positions, channels)
        for a in range(3)
        for b in range(3)
    ]
    tap_rows = jnp.concatenate(taps, axis=-1)

    half = jnp.concatenate(pieces, axis=0)
    whole = jnp.concatenate([half, lax.ppermute(half, "lon", CORES)], axis=0)
    summed = lax.dot_general(
        tap_rows, whole, (((1,), (1,)), ((), ())), preferred_element_type=jnp.float32
    )
    hidden = jax.nn.silu(summed + own_order(spatial_bias, 0)).astype(jnp.bfloat16)
    hidden = hidden.reshape(lon_cols, frames, lat_rows, channels)

    up = [(i, i + 1) for i in range(FRAMES_AXIS - 1)]
    down = [(i + 1, i) for i in range(FRAMES_AXIS - 1)]
    earlier = lax.ppermute(hidden[:, -1:], "frame", up)
    later = lax.ppermute(hidden[:, :1], "frame", down)
    framed = jnp.concatenate([earlier, hidden, later], axis=1)
    stacked = jnp.concatenate([framed[:, k : k + frames] for k in range(3)], axis=-1)
    ordered = own_order(temporal_kernel.reshape(3, channels, channels), 1)
    mixed = jnp.dot(
        stacked.reshape(-1, 3 * channels),
        ordered.reshape(3 * channels, channels),
        preferred_element_type=jnp.float32,
    )
    mixed = (mixed + temporal_bias).reshape(lon_cols, frames, lat_rows, channels)
    result = columns.astype(jnp.float32) + jax.nn.silu(mixed)
    return result.astype(jnp.bfloat16).transpose(1, 2, 0, 3)


def solution(mesh):
    placed = (P("frame", None, "lon", None), P("frame", "lon"), P(), P(), P())
    return jax.shard_map(
        body, mesh=mesh, in_specs=placed, out_specs=P("frame", None, "lon", None), check_vma=False
    )
```

```python
import jax
import jax.numpy as jnp
import numpy as np
from jax import lax
from jax.sharding import PartitionSpec as P

LONS = 16
FRAMES_AXIS = 32
Y = 4
X = 4
Z_LO = 8


def lon_index(y, z_hi, core):
    return y * 4 + z_hi * 2 + core


def frame_index(x, z_lo):
    return x * Z_LO + z_lo


def z_groups():
    return [
        [
            lon_index(y, z_hi, core) * FRAMES_AXIS + frame_index(x, z_lo)
            for z_hi in range(2)
            for z_lo in range(Z_LO)
        ]
        for x in range(X)
        for y in range(Y)
        for core in range(2)
    ]


def x_groups():
    return [[frame_index(x, z_lo) for x in range(X)] for z_lo in range(Z_LO)]


def from_y(k):
    return [(((y + k) % Y) * 4 + r, y * 4 + r) for y in range(Y) for r in range(4)]


CORES = [(i, i ^ 1) for i in range(LONS)]
FAR = [(i, (i + 1) % LONS if i % 2 else (i - 1) % LONS) for i in range(LONS)]

ARRIVALS = (
    ((0, 0), (0, 1)),
    ((3, 0), (1, 1)),
    ((3, 1), (1, 0)),
    ((2, 0), (2, 1)),
)


def copies(piece, count):
    return jnp.broadcast_to(piece[None], (count,) + piece.shape)


def gather_rows(spatial_kernel):
    shard = spatial_kernel.T
    cols, rows = shard.shape
    along_z = lax.all_to_all(
        copies(shard, 16), ("lon", "frame"), 0, 0, axis_index_groups=z_groups()
    )
    along_z = along_z.reshape(2, Z_LO, cols, rows).transpose(0, 2, 1, 3)
    along_z = along_z.reshape(2 * cols, Z_LO * rows)
    along_x = lax.all_to_all(copies(along_z, X), "frame", 0, 0, axis_index_groups=x_groups())
    return jnp.concatenate([along_x[x] for x in range(X)], axis=1)


def arrival_order():
    lon = lax.axis_index("lon")
    blocks = [(k, z_hi, side) for arrival in ARRIVALS for side in range(2) for k, z_hi in arrival]
    ahead, z_hi, side = (jnp.asarray(np.repeat(np.array(v), 40)) for v in zip(*blocks))
    within = jnp.asarray(np.tile(np.arange(40), LONS))
    row = lax.rem(lon // 4 + ahead, Y)
    return lon_index(row, z_hi, (lon % 2) ^ side) * 40 + within


def gather_arrivals(mine):
    half = mine.shape[0] // 2
    low, high = mine[:half], mine[half:]
    low_behind = lax.ppermute(low, "lon", from_y(3))
    high_ahead = lax.ppermute(high, "lon", from_y(1))
    high_behind = lax.ppermute(high, "lon", from_y(3))
    low_ahead = lax.ppermute(low, "lon", from_y(1))
    low_across = lax.ppermute(low_behind, "lon", from_y(3))
    high_across = lax.ppermute(high_ahead, "lon", from_y(1))
    arrivals = [
        mine,
        jnp.concatenate([low_behind, high_ahead]),
        jnp.concatenate([high_behind, low_ahead]),
        jnp.concatenate([low_across, high_across]),
    ]
    return [(own, lax.ppermute(own, "lon", CORES)) for own in arrivals]


def widened(latents):
    core = lax.axis_index("lon") % 2
    columns = latents.transpose(2, 0, 1, 3)
    far = lax.ppermute(jnp.where(core == 1, columns[-1], columns[0]), "lon", FAR)
    near = lax.ppermute(jnp.where(core == 1, columns[0], columns[-1]), "lon", CORES)
    before = jnp.where(core == 1, near, far)
    after = jnp.where(core == 1, far, near)
    return columns, jnp.concatenate([before[None], columns, after[None]], axis=0)


def with_frames(wide):
    up = [(i, i + 1) for i in range(FRAMES_AXIS - 1)]
    down = [(i + 1, i) for i in range(FRAMES_AXIS - 1)]
    earlier = lax.ppermute(wide[:, -1:], "frame", up)
    later = lax.ppermute(wide[:, :1], "frame", down)
    return jnp.concatenate([earlier, wide, later], axis=1)


def body(latents, spatial_kernel, spatial_bias, temporal_kernel, temporal_bias):
    frames, lat_rows, lon_cols, channels = latents.shape
    columns, wide = widened(latents)
    mine = gather_rows(spatial_kernel)
    mine, wide, temporal_kernel = lax.optimization_barrier((mine, wide, temporal_kernel))
    arrivals = gather_arrivals(mine)

    wide = jnp.pad(with_frames(wide), ((0, 0), (0, 0), (1, 1), (0, 0)))
    taps = [
        wide[b : b + lon_cols, :, a : a + lat_rows].reshape(-1, channels)
        for a in range(3)
        for b in range(3)
    ]
    tap_rows = jnp.concatenate(taps, axis=-1)

    frame = lax.axis_index("frame")
    step = lax.broadcasted_iota(jnp.int32, (lon_cols, frames + 2, lat_rows, 1), 1)
    outside = ((step == 0) & (frame == 0)) | ((step == frames + 1) & (frame == FRAMES_AXIS - 1))
    outside = outside.reshape(-1, 1)
    order = arrival_order()[:, None] == lax.broadcasted_iota(jnp.int32, (channels, channels), 1)
    bias = jnp.sum(jnp.where(order, spatial_bias[None, :], 0.0), axis=1)
    parts, start = [], 0
    for group in (arrivals[:3], arrivals[3:]):
        rows = jnp.concatenate([piece for pair in group for piece in pair], axis=0)
        summed = lax.dot_general(
            tap_rows, rows, (((1,), (1,)), ((), ())), preferred_element_type=jnp.float32
        )
        active = jax.nn.silu(summed + bias[start : start + rows.shape[0]])
        parts.append(jnp.where(outside, 0.0, active).astype(jnp.bfloat16))
        start += rows.shape[0]
    hidden = jnp.concatenate(parts, axis=-1)
    hidden = hidden.reshape(lon_cols, frames + 2, lat_rows, channels)

    stacked = jnp.concatenate([hidden[:, k : k + frames] for k in range(3)], axis=-1)
    ordered = [
        jnp.dot(order.astype(jnp.bfloat16), temporal_kernel[k * channels : (k + 1) * channels])
        for k in range(3)
    ]
    mixed = jnp.dot(
        stacked.reshape(-1, 3 * channels),
        jnp.concatenate(ordered, axis=0),
        preferred_element_type=jnp.float32,
    )
    mixed = (mixed + temporal_bias).reshape(lon_cols, frames, lat_rows, channels)
    result = columns.astype(jnp.float32) + jax.nn.silu(mixed)
    return result.astype(jnp.bfloat16).transpose(1, 2, 0, 3)


def solution(mesh):
    placed = (P("frame", None, "lon", None), P("frame", "lon"), P(), P(), P())
    return jax.shard_map(
        body, mesh=mesh, in_specs=placed, out_specs=P("frame", None, "lon", None), check_vma=False
    )
```

```python
import jax
import jax.numpy as jnp
import numpy as np
from jax import lax
from jax.sharding import PartitionSpec as P

LONS = 16
FRAMES_AXIS = 32
Y = 4
X = 4
Z_LO = 8


def lon_index(y, z_hi, core):
    return y * 4 + z_hi * 2 + core


def frame_index(x, z_lo):
    return x * Z_LO + z_lo


def z_groups():
    return [
        [
            lon_index(y, z_hi, core) * FRAMES_AXIS + frame_index(x, z_lo)
            for z_hi in range(2)
            for z_lo in range(Z_LO)
        ]
        for x in range(X)
        for y in range(Y)
        for core in range(2)
    ]


def x_groups():
    return [[frame_index(x, z_lo) for x in range(X)] for z_lo in range(Z_LO)]


def from_y(k):
    return [(((y + k) % Y) * 4 + r, y * 4 + r) for y in range(Y) for r in range(4)]


CORES = [(i, i ^ 1) for i in range(LONS)]
FAR = [(i, (i + 1) % LONS if i % 2 else (i - 1) % LONS) for i in range(LONS)]


def copies(piece, count):
    return jnp.broadcast_to(piece[None], (count,) + piece.shape)


def gather_z(spatial_kernel):
    shard = spatial_kernel.T
    cols, rows = shard.shape
    along_z = lax.all_to_all(
        copies(shard, 16), ("lon", "frame"), 0, 0, axis_index_groups=z_groups()
    )
    along_z = along_z.reshape(2, Z_LO, cols, rows)
    return [jnp.concatenate([along_z[h, z] for z in range(Z_LO)], axis=1) for h in range(2)]


def over_x(block):
    return lax.all_to_all(copies(block, X), "frame", 0, 0, axis_index_groups=x_groups())


def over_y(block):
    return [block] + [lax.ppermute(block, "lon", from_y(k)) for k in (1, 2, 3)]


def joined_rows(along_x):
    return jnp.concatenate([along_x[x] for x in range(X)], axis=1)


def channel_order():
    lon = lax.axis_index("lon")
    blocks = [(y, z_hi, side) for side in range(2) for z_hi in range(2) for y in range(Y)]
    row, z_hi, side = (jnp.asarray(np.repeat(np.array(v), 40)) for v in zip(*blocks))
    within = jnp.asarray(np.tile(np.arange(40), LONS))
    row = lax.rem(lon // 4 + row, Y)
    return lon_index(row, z_hi, (lon % 2) ^ side) * 40 + within


def lon_halos(columns):
    core = lax.axis_index("lon") % 2
    far = lax.ppermute(jnp.where(core == 1, columns[-1], columns[0]), "lon", FAR)
    near = lax.ppermute(jnp.where(core == 1, columns[0], columns[-1]), "lon", CORES)
    return far, near


def frame_halos(wide):
    up = [(i, i + 1) for i in range(FRAMES_AXIS - 1)]
    down = [(i + 1, i) for i in range(FRAMES_AXIS - 1)]
    earlier = lax.ppermute(wide[:, -1:], "frame", up)
    later = lax.ppermute(wide[:, :1], "frame", down)
    return earlier, later


def tap_rows(wide, lon_cols, lat_rows):
    padded = jnp.pad(wide, ((0, 0), (0, 0), (1, 1), (0, 0)))
    taps = [
        padded[b : b + lon_cols, :, a : a + lat_rows].reshape(-1, padded.shape[-1])
        for a in range(3)
        for b in range(3)
    ]
    return jnp.concatenate(taps, axis=-1)


def active(rows, kernel_rows, bias):
    summed = lax.dot_general(
        rows, kernel_rows, (((1,), (1,)), ((), ())), preferred_element_type=jnp.float32
    )
    return jax.nn.silu(summed + bias)


def body(latents, spatial_kernel, spatial_bias, temporal_kernel, temporal_bias):
    frames, lat_rows, lon_cols, channels = latents.shape
    core = lax.axis_index("lon") % 2
    columns = latents.transpose(2, 0, 1, 3)
    far, near = lon_halos(columns)
    low, high = gather_z(spatial_kernel)
    high = jnp.concatenate(over_y(high))
    low = joined_rows(over_x(low))
    _, _, temporal_kernel = lax.optimization_barrier((low, high, temporal_kernel))
    low = over_y(low)
    high = over_x(high)
    far, near, columns, _ = lax.optimization_barrier((far, near, columns, low[1]))
    low = jnp.concatenate(low)

    order = channel_order()[:, None] == lax.broadcasted_iota(jnp.int32, (channels, channels), 1)
    ordered = [
        jnp.dot(order.astype(jnp.bfloat16), temporal_kernel[k * channels : (k + 1) * channels])
        for k in range(3)
    ]
    ordered = jnp.concatenate(ordered, axis=0)
    bias = jnp.sum(jnp.where(order, spatial_bias[None, :], 0.0), axis=1)

    before = jnp.where(core == 1, near, far)
    after = jnp.where(core == 1, far, near)
    wide = jnp.concatenate([before[None], columns, after[None]], axis=0)
    inner_rows = tap_rows(wide, lon_cols, lat_rows)
    earlier, later = frame_halos(wide)

    other_low = lax.ppermute(low, "lon", CORES)
    other_high = joined_rows(lax.ppermute(high, "lon", CORES))
    middle = jnp.concatenate([joined_rows(high), other_low])
    groups = (low, middle, other_high)
    ends = np.cumsum([rows.shape[0] for rows in groups])
    biases = [bias[end - rows.shape[0] : end] for rows, end in zip(groups, ends)]
    inner = [active(inner_rows, rows, part) for rows, part in zip(groups[:2], biases)]
    earlier, later, inner[1] = lax.optimization_barrier((earlier, later, inner[1]))
    outer_rows = tap_rows(jnp.concatenate([earlier, later], axis=1), lon_cols, lat_rows)
    outer = [active(outer_rows, rows, part) for rows, part in zip(groups, biases)]
    inner.append(active(inner_rows, groups[2], biases[2]))

    inner = jnp.concatenate(inner, axis=-1).astype(jnp.bfloat16)
    inner = inner.reshape(lon_cols, frames, lat_rows, channels)
    outer = jnp.concatenate(outer, axis=-1).astype(jnp.bfloat16)
    outer = outer.reshape(lon_cols, 2, lat_rows, channels)
    frame = lax.axis_index("frame")
    first = jnp.where(frame == 0, 0, outer[:, :1])
    final = jnp.where(frame == FRAMES_AXIS - 1, 0, outer[:, 1:])
    hidden = jnp.concatenate([first, inner, final], axis=1)

    stacked = jnp.concatenate([hidden[:, k : k + frames] for k in range(3)], axis=-1)
    mixed = jnp.dot(
        stacked.reshape(-1, 3 * channels), ordered, preferred_element_type=jnp.float32
    )
    mixed = (mixed + temporal_bias).reshape(lon_cols, frames, lat_rows, channels)
    result = columns.astype(jnp.float32) + jax.nn.silu(mixed)
    return result.astype(jnp.bfloat16).transpose(1, 2, 0, 3)


def solution(mesh):
    placed = (P("frame", None, "lon", None), P("frame", "lon"), P(), P(), P())
    return jax.shard_map(
        body, mesh=mesh, in_specs=placed, out_specs=P("frame", None, "lon", None), check_vma=False
    )
```

```python
import jax
import jax.numpy as jnp
import numpy as np
from jax import lax
from jax.experimental import pallas as pl
from jax.experimental.pallas import tpu as pltpu
from jax.sharding import PartitionSpec as P

LONS = 16
FRAMES_AXIS = 32
Y = 4
X = 4
Z_LO = 8


def lon_index(y, z_hi, core):
    return y * 4 + z_hi * 2 + core


def frame_index(x, z_lo):
    return x * Z_LO + z_lo


def z_groups():
    return [
        [
            lon_index(y, z_hi, core) * FRAMES_AXIS + frame_index(x, z_lo)
            for z_hi in range(2)
            for z_lo in range(Z_LO)
        ]
        for x in range(X)
        for y in range(Y)
        for core in range(2)
    ]


def x_groups():
    return [[frame_index(x, z_lo) for x in range(X)] for z_lo in range(Z_LO)]


def across_y(k):
    return [((y ^ k) * 4 + r, y * 4 + r) for y in range(Y) for r in range(4)]


CORES = [(i, i ^ 1) for i in range(LONS)]
FAR = [(i, (i + 1) % LONS if i % 2 else (i - 1) % LONS) for i in range(LONS)]


def copies(piece, count):
    return jnp.broadcast_to(piece[None], (count,) + piece.shape)


def gather_z(spatial_kernel):
    shard = spatial_kernel.T
    cols, rows = shard.shape
    along_z = lax.all_to_all(
        copies(shard, 16), ("lon", "frame"), 0, 0, axis_index_groups=z_groups()
    )
    along_z = along_z.reshape(2, Z_LO, cols, rows)
    return [jnp.concatenate([along_z[h, z] for z in range(Z_LO)], axis=1) for h in range(2)]


def over_x(block):
    return lax.all_to_all(copies(block, X), "frame", 0, 0, axis_index_groups=x_groups())


def doubled_over_y(block):
    block = jnp.concatenate([block, lax.ppermute(block, "lon", across_y(1))])
    return jnp.concatenate([block, lax.ppermute(block, "lon", across_y(3))])


def over_y(block):
    return [block] + [lax.ppermute(block, "lon", across_y(k)) for k in (1, 3, 2)]


def join_kernel(parts_ref, joined_ref):
    parts, _, width = parts_ref.shape
    for x in range(parts):
        joined_ref[:, x * width : (x + 1) * width] = parts_ref[x]


def joined_rows(along_x):
    parts, count, width = along_x.shape
    return pl.pallas_call(
        join_kernel,
        out_shape=jax.ShapeDtypeStruct((count, parts * width), along_x.dtype),
        in_specs=[pl.BlockSpec(memory_space=pltpu.VMEM)],
        out_specs=pl.BlockSpec(memory_space=pltpu.VMEM),
        compiler_params=pltpu.CompilerParams(vmem_limit_bytes=12 * 1024 * 1024),
        cost_estimate=pl.CostEstimate(flops=0, bytes_accessed=2 * 2 * along_x.size, transcendentals=0),
    )(along_x)


def channel_order():
    lon = lax.axis_index("lon")
    blocks = [(k, z_hi, side) for z_hi, side in ((0, 0), (0, 1), (1, 0), (1, 1)) for k in (0, 1, 3, 2)]
    row, z_hi, side = (jnp.asarray(np.repeat(np.array(v), 40)) for v in zip(*blocks))
    within = jnp.asarray(np.tile(np.arange(40), LONS))
    return lon_index((lon // 4) ^ row, z_hi, (lon % 2) ^ side) * 40 + within


def lon_halos(columns):
    core = lax.axis_index("lon") % 2
    far = lax.ppermute(jnp.where(core == 1, columns[-1], columns[0]), "lon", FAR)
    near = lax.ppermute(jnp.where(core == 1, columns[0], columns[-1]), "lon", CORES)
    return far, near


def frame_halos(wide):
    up = [(i, i + 1) for i in range(FRAMES_AXIS - 1)]
    down = [(i + 1, i) for i in range(FRAMES_AXIS - 1)]
    earlier = lax.ppermute(wide[:, -1:], "frame", up)
    later = lax.ppermute(wide[:, :1], "frame", down)
    return earlier, later


def tap_rows(wide, lon_cols, lat_rows):
    padded = jnp.pad(wide, ((0, 0), (0, 0), (1, 1), (0, 0)))
    taps = [
        padded[b : b + lon_cols, :, a : a + lat_rows].reshape(-1, padded.shape[-1])
        for a in range(3)
        for b in range(3)
    ]
    return jnp.concatenate(taps, axis=-1)


def active(rows, kernel_rows, bias):
    summed = lax.dot_general(
        rows, kernel_rows, (((1,), (1,)), ((), ())), preferred_element_type=jnp.float32
    )
    return jax.nn.silu(summed + bias)


def body(latents, spatial_kernel, spatial_bias, temporal_kernel, temporal_bias):
    frames, lat_rows, lon_cols, channels = latents.shape
    core = lax.axis_index("lon") % 2
    columns = latents.transpose(2, 0, 1, 3)
    far, near = lon_halos(columns)
    low, high = gather_z(spatial_kernel)
    _, temporal_kernel = lax.optimization_barrier((low, temporal_kernel))
    high = doubled_over_y(high)
    low = joined_rows(over_x(low))
    low = over_y(low)
    high = over_x(high)
    far, near, columns, _ = lax.optimization_barrier((far, near, columns, low[1]))
    other_high = joined_rows(lax.ppermute(high, "lon", CORES))

    before = jnp.where(core == 1, near, far)
    after = jnp.where(core == 1, far, near)
    wide = jnp.concatenate([before[None], columns, after[None]], axis=0)
    earlier, later = frame_halos(wide)
    inner_taps = tap_rows(wide, lon_cols, lat_rows)
    earlier, later, *low = lax.optimization_barrier((earlier, later, *low))
    low = jnp.concatenate(low)
    other_low = lax.ppermute(low, "lon", CORES)
    halo_taps = tap_rows(jnp.concatenate([earlier, later], axis=1), lon_cols, lat_rows)
    taps = jnp.concatenate([inner_taps, halo_taps], axis=0)

    order = channel_order()[:, None] == lax.broadcasted_iota(jnp.int32, (channels, channels), 1)
    ordered = [
        jnp.dot(order.astype(jnp.bfloat16), temporal_kernel[k * channels : (k + 1) * channels])
        for k in range(3)
    ]
    ordered = jnp.concatenate(ordered, axis=0)
    bias = jnp.sum(jnp.where(order, spatial_bias[None, :], 0.0), axis=1)

    early = jnp.concatenate([low, other_low, joined_rows(high)])
    split = early.shape[0]
    hidden = [active(taps, early, bias[:split]), active(taps, other_high, bias[split:])]
    hidden = jnp.concatenate(hidden, axis=-1).astype(jnp.bfloat16)
    inner_size = lon_cols * frames * lat_rows
    inner = hidden[:inner_size].reshape(lon_cols, frames, lat_rows, channels)
    halo = hidden[inner_size:].reshape(lon_cols, 2, lat_rows, channels)
    frame = lax.axis_index("frame")
    first = jnp.where(frame == 0, 0, halo[:, :1])
    final = jnp.where(frame == FRAMES_AXIS - 1, 0, halo[:, 1:])
    hidden = jnp.concatenate([first, inner, final], axis=1)

    stacked = jnp.concatenate([hidden[:, k : k + frames] for k in range(3)], axis=-1)
    mixed = jnp.dot(
        stacked.reshape(-1, 3 * channels), ordered, preferred_element_type=jnp.float32
    )
    mixed = (mixed + temporal_bias).reshape(lon_cols, frames, lat_rows, channels)
    result = columns.astype(jnp.float32) + jax.nn.silu(mixed)
    return result.astype(jnp.bfloat16).transpose(1, 2, 0, 3)


def solution(mesh):
    placed = (P("frame", None, "lon", None), P("frame", "lon"), P(), P(), P())
    return jax.shard_map(
        body, mesh=mesh, in_specs=placed, out_specs=P("frame", None, "lon", None), check_vma=False
    )
```

```python
import functools

import jax
import jax.numpy as jnp
import numpy as np
from jax import lax
from jax.experimental import pallas as pl
from jax.experimental.pallas import tpu as pltpu
from jax.sharding import PartitionSpec as P

LONS = 16
FRAMES_AXIS = 32
Y = 4
X = 4
Z_LO = 8


def lon_index(y, z_hi, core):
    return y * 4 + z_hi * 2 + core


def frame_index(x, z_lo):
    return x * Z_LO + z_lo


def z_groups():
    return [
        [
            lon_index(y, z_hi, core) * FRAMES_AXIS + frame_index(x, z_lo)
            for z_hi in range(2)
            for z_lo in range(Z_LO)
        ]
        for x in range(X)
        for y in range(Y)
        for core in range(2)
    ]


def x_groups():
    return [[frame_index(x, z_lo) for x in range(X)] for z_lo in range(Z_LO)]


def across_y(k):
    return [((y ^ k) * 4 + r, y * 4 + r) for y in range(Y) for r in range(4)]


NEAR_FIRST = (0, 1, 3, 2)
CORES = [(i, i ^ 1) for i in range(LONS)]


def far_steps():
    first, second = [], []
    for lon in range(LONS):
        y, z_hi, core = lon // 4, lon // 2 % 2, lon % 2
        target = (lon + 1) % LONS if core else (lon - 1) % LONS
        for frame in range(FRAMES_AXIS):
            x, z_lo = frame // Z_LO, frame % Z_LO
            z = (z_hi * Z_LO + z_lo + (4 if core else 12)) % 16
            relay = lon_index(y, z // Z_LO, core) * FRAMES_AXIS + frame_index(x, z % Z_LO)
            first.append((lon * FRAMES_AXIS + frame, relay))
            second.append((relay, target * FRAMES_AXIS + frame))
    return first, second


def across_x(k):
    return [
        (frame_index(x ^ k, z_lo), frame_index(x, z_lo)) for x in range(X) for z_lo in range(Z_LO)
    ]


def copies(piece, count):
    return jnp.broadcast_to(piece[None], (count,) + piece.shape)


def gather_z(spatial_kernel):
    shard = spatial_kernel.T
    cols, rows = shard.shape
    along_z = lax.all_to_all(
        copies(shard, 16), ("lon", "frame"), 0, 0, axis_index_groups=z_groups()
    )
    along_z = along_z.reshape(2, Z_LO, cols, rows)
    return [jnp.concatenate([along_z[h, z] for z in range(Z_LO)], axis=1) for h in range(2)]


def over_x(block):
    return lax.all_to_all(copies(block, X), "frame", 0, 0, axis_index_groups=x_groups())


def doubled_over_y(block):
    block = jnp.concatenate([block, lax.ppermute(block, "lon", across_y(1))])
    return jnp.concatenate([block, lax.ppermute(block, "lon", across_y(3))])


def over_y(block):
    return [block] + [lax.ppermute(block, "lon", across_y(k)) for k in NEAR_FIRST[1:]]


def piecewise_over_x(block):
    return [block] + [lax.ppermute(block, "frame", across_x(k)) for k in NEAR_FIRST[1:]]


def joined_x(along_x):
    return jnp.concatenate([along_x[x] for x in range(X)], axis=1)


def channel_order():
    lon = lax.axis_index("lon")
    blocks = [(k, z_hi, side) for z_hi, side in ((0, 0), (0, 1), (1, 0), (1, 1)) for k in NEAR_FIRST]
    row, z_hi, side = (jnp.asarray(np.repeat(np.array(v), 40)) for v in zip(*blocks))
    within = jnp.asarray(np.tile(np.arange(40), LONS))
    return lon_index((lon // 4) ^ row, z_hi, (lon % 2) ^ side) * 40 + within


def lon_halos(columns):
    core = lax.axis_index("lon") % 2
    first, _ = far_steps()
    far = lax.ppermute(jnp.where(core == 1, columns[-1], columns[0]), ("lon", "frame"), first)
    near = lax.ppermute(jnp.where(core == 1, columns[0], columns[-1]), "lon", CORES)
    return far, near


def frame_halos(wide):
    up = [(i, i + 1) for i in range(FRAMES_AXIS - 1)]
    down = [(i + 1, i) for i in range(FRAMES_AXIS - 1)]
    earlier = lax.ppermute(wide[:, -1:], "frame", up)
    later = lax.ppermute(wide[:, :1], "frame", down)
    return earlier, later


VMEM = pl.BlockSpec(memory_space=pltpu.VMEM)
SMEM = pl.BlockSpec(memory_space=pltpu.SMEM)
ANY = pl.BlockSpec(memory_space=pl.ANY)


def params(mebibytes):
    return pltpu.CompilerParams(vmem_limit_bytes=mebibytes * 2**20)


def order_kernel(order_ref, kernel_ref, out_ref):
    channels = order_ref.shape[0]
    for k in range(3):
        part = slice(k * channels, (k + 1) * channels)
        moved = jnp.dot(order_ref[...], kernel_ref[part], preferred_element_type=jnp.float32)
        out_ref[part] = moved.astype(jnp.bfloat16)


def shift_rows(planes_ref, taps_ref, lat_rows):
    planes, rows, channels = planes_ref.shape
    row = lax.rem(lax.broadcasted_iota(jnp.int32, (rows, channels), 0), lat_rows)

    def plane(p, carry):
        here = planes_ref[p]
        wider = here.astype(jnp.float32)
        above = jnp.where(row == 0, 0.0, pltpu.roll(wider, 1, 0))
        below = jnp.where(row == lat_rows - 1, 0.0, pltpu.roll(wider, rows - 1, 0))
        taps_ref[0, p] = above.astype(jnp.bfloat16)
        taps_ref[1, p] = here
        taps_ref[2, p] = below.astype(jnp.bfloat16)
        return carry

    lax.fori_loop(0, planes, plane, 0)


def join_rows(parts_ref, joined_ref):
    parts, _, width = parts_ref.shape
    for x in range(parts):
        joined_ref[:, x * width : (x + 1) * width] = parts_ref[x]


def silu(v):
    return v * jax.nn.sigmoid(v)


def block_kernel(
    lat_rows, flags_ref, planes_any, low_any, other_low_any, h0, h1, h2, h3, o0, o1, o2, o3,
    kernel_any, bias_ref, tbias_ref, out_ref, planes_ref, low_ref, other_low_ref, high_ref,
    other_high_ref, kernel_ref, taps_ref, joined_ref, other_joined_ref, sems,
):
    x = lax.axis_index("frame") // Z_LO
    pairs = [(planes_any, planes_ref)]
    pairs += [(part, high_ref.at[x ^ k]) for k, part in zip(NEAR_FIRST, (h0, h1, h2, h3))]
    pairs += [(part, other_high_ref.at[x ^ k]) for k, part in zip(NEAR_FIRST, (o0, o1, o2, o3))]
    pairs += [(low_any, low_ref), (other_low_any, other_low_ref), (kernel_any, kernel_ref)]
    moves = [
        pltpu.make_async_copy(source, target, sems.at[i])
        for i, (source, target) in enumerate(pairs)
    ]
    for move in moves:
        move.start()
    moves[0].wait()
    shift_rows(planes_ref, taps_ref, lat_rows)
    for move in moves[1:5]:
        move.wait()
    join_rows(high_ref, joined_ref)
    for move in moves[5:9]:
        move.wait()
    join_rows(other_high_ref, other_joined_ref)
    moves[9].wait()
    moves[10].wait()

    planes, rows, channels = planes_ref.shape
    columns, inner = planes - 2, rows - 2 * lat_rows
    total = None
    for a in range(3):
        taps = [taps_ref[a, b : b + columns].reshape(columns * rows, channels) for b in range(3)]
        part = slice(3 * a * channels, 3 * (a + 1) * channels)
        weights = [r[:, part] for r in (low_ref, other_low_ref, joined_ref, other_joined_ref)]
        term = lax.dot_general(
            jnp.concatenate(taps, axis=1),
            jnp.concatenate(weights, axis=0),
            (((1,), (1,)), ((), ())),
            preferred_element_type=jnp.float32,
        )
        total = term if total is None else total + term
    active = silu(total + bias_ref[...])
    row = lax.rem(lax.broadcasted_iota(jnp.int32, active.shape, 0), rows)
    outside = (row < lat_rows) & (flags_ref[0] == 1)
    outside = outside | ((row >= rows - lat_rows) & (flags_ref[1] == 1))
    hidden = jnp.where(outside, 0.0, active).astype(jnp.bfloat16).reshape(columns, rows, channels)
    stacked = [
        hidden[:, k * lat_rows : k * lat_rows + inner].reshape(columns * inner, channels)
        for k in range(3)
    ]
    moves[11].wait()
    mixed = jnp.dot(
        jnp.concatenate(stacked, axis=1), kernel_ref[...], preferred_element_type=jnp.float32
    )
    mixed = silu(mixed + tbias_ref[...]).reshape(columns, inner, channels)
    here = planes_ref[1 : planes - 1, lat_rows : lat_rows + inner].astype(jnp.float32)
    out_ref[...] = (here + mixed).astype(jnp.bfloat16)


def block(flags, planes, low, other_low, high, other_high, kernel, bias, tbias, lat_rows):
    count, rows, channels = planes.shape
    inner = rows - 2 * lat_rows
    moved = (planes, low, other_low, *high, *other_high, kernel)
    parts = (len(high), *high[0].shape)
    shapes = (planes.shape, low.shape, low.shape, parts, parts, kernel.shape)
    shapes += ((3, *planes.shape), low.shape, low.shape)
    flops = (count - 2) * 2 * channels * channels * (9 * rows + 3 * inner)
    return pl.pallas_call(
        functools.partial(block_kernel, lat_rows),
        out_shape=jax.ShapeDtypeStruct((count - 2, inner, channels), jnp.bfloat16),
        in_specs=[SMEM] + [ANY] * len(moved) + [VMEM, VMEM],
        out_specs=VMEM,
        scratch_shapes=[pltpu.VMEM(s, jnp.bfloat16) for s in shapes]
        + [pltpu.SemaphoreType.DMA((len(moved),))],
        compiler_params=params(34),
        cost_estimate=pl.CostEstimate(flops=flops, bytes_accessed=2**24, transcendentals=0),
    )(flags, *moved, bias, tbias)


def reordered(order, kernel):
    return pl.pallas_call(
        order_kernel,
        out_shape=jax.ShapeDtypeStruct(kernel.shape, jnp.bfloat16),
        in_specs=[VMEM, VMEM],
        out_specs=VMEM,
        compiler_params=params(16),
        cost_estimate=pl.CostEstimate(
            flops=2 * kernel.size * order.shape[0], bytes_accessed=2**23, transcendentals=0
        ),
    )(order, kernel)


def body(latents, spatial_kernel, spatial_bias, temporal_kernel, temporal_bias):
    frames, lat_rows, lon_cols, channels = latents.shape
    core = lax.axis_index("lon") % 2
    columns = latents.transpose(2, 0, 1, 3)
    far, near = lon_halos(columns)
    low, high = gather_z(spatial_kernel)
    far, near, low, high = lax.optimization_barrier((far, near, low, high))
    far = lax.ppermute(far, ("lon", "frame"), far_steps()[1])
    high = doubled_over_y(high)
    low = joined_x(over_x(low))
    far, near, columns, temporal_kernel, low, high = lax.optimization_barrier(
        (far, near, columns, temporal_kernel, low, high)
    )
    low = over_y(low)
    high = piecewise_over_x(high)
    before = jnp.where(core == 1, near, far)
    after = jnp.where(core == 1, far, near)
    wide = jnp.concatenate([before[None], columns, after[None]], axis=0)
    earlier, later = frame_halos(wide)
    other_own = lax.ppermute(high[0], "lon", CORES)
    low = jnp.concatenate(low)
    order = channel_order()[:, None] == lax.broadcasted_iota(jnp.int32, (channels, channels), 1)
    bias = jnp.sum(jnp.where(order, spatial_bias[None, :], 0.0), axis=1)
    ordered = reordered(order.astype(jnp.bfloat16), temporal_kernel)
    earlier, later, low, ordered, bias, *_ = lax.optimization_barrier(
        (earlier, later, low, ordered, bias, *high)
    )
    other_high = [other_own] + [lax.ppermute(part, "lon", CORES) for part in high[1:]]
    planes = jnp.concatenate([earlier, wide, later], axis=1)
    planes = planes.reshape(lon_cols + 2, (frames + 2) * lat_rows, channels)
    other_low = lax.ppermute(low, "lon", CORES)

    frame = lax.axis_index("frame")
    flags = jnp.stack([frame == 0, frame == FRAMES_AXIS - 1]).astype(jnp.int32)
    result = block(
        flags, planes, low, other_low, high, other_high, ordered, bias[None],
        temporal_bias[None], lat_rows,
    )
    return result.reshape(lon_cols, frames, lat_rows, channels).transpose(1, 2, 0, 3)


def solution(mesh):
    placed = (P("frame", None, "lon", None), P("frame", "lon"), P(), P(), P())
    return jax.shard_map(
        body, mesh=mesh, in_specs=placed, out_specs=P("frame", None, "lon", None), check_vma=False
    )
```

```python
import functools

import jax
import jax.numpy as jnp
import numpy as np
from jax import lax
from jax.experimental import pallas as pl
from jax.experimental.pallas import tpu as pltpu
from jax.sharding import PartitionSpec as P

LONS = 16
FRAMES_AXIS = 32
Y = 4
X = 4
Z_LO = 8


def lon_index(y, z_hi, core):
    return y * 4 + z_hi * 2 + core


def frame_index(x, z_lo):
    return x * Z_LO + z_lo


def z_groups():
    return [
        [
            lon_index(y, z_hi, core) * FRAMES_AXIS + frame_index(x, z_lo)
            for z_hi in range(2)
            for z_lo in range(Z_LO)
        ]
        for x in range(X)
        for y in range(Y)
        for core in range(2)
    ]


def x_groups():
    return [[frame_index(x, z_lo) for x in range(X)] for z_lo in range(Z_LO)]


def across_y(k):
    return [((y ^ k) * 4 + r, y * 4 + r) for y in range(Y) for r in range(4)]


NEAR_FIRST = (0, 1, 3, 2)
CORES = [(i, i ^ 1) for i in range(LONS)]
FAR = [(i, (i + 1) % LONS if i % 2 else (i - 1) % LONS) for i in range(LONS)]


def copies(piece, count):
    return jnp.broadcast_to(piece[None], (count,) + piece.shape)


def gather_z(spatial_kernel):
    shard = spatial_kernel.T
    cols, rows = shard.shape
    along_z = lax.all_to_all(
        copies(shard, 16), ("lon", "frame"), 0, 0, axis_index_groups=z_groups()
    )
    along_z = along_z.reshape(2, Z_LO, cols, rows).transpose(0, 2, 1, 3)
    return along_z.reshape(2 * cols, Z_LO * rows)


def over_x(block):
    return lax.all_to_all(copies(block, X), "frame", 0, 0, axis_index_groups=x_groups())


def over_y(block):
    return [block] + [lax.ppermute(block, "lon", across_y(k)) for k in NEAR_FIRST[1:]]


def joined_x(along_x):
    return jnp.concatenate([along_x[x] for x in range(X)], axis=1)


def channel_order():
    lon = lax.axis_index("lon")
    blocks = [(k, side, z_hi) for k in NEAR_FIRST for side in range(2) for z_hi in range(2)]
    row, side, z_hi = (jnp.asarray(np.repeat(np.array(v), 40)) for v in zip(*blocks))
    within = jnp.asarray(np.tile(np.arange(40), LONS))
    return lon_index((lon // 4) ^ row, z_hi, (lon % 2) ^ side) * 40 + within


def lon_halos(columns):
    core = lax.axis_index("lon") % 2
    far = lax.ppermute(jnp.where(core == 1, columns[-1], columns[0]), "lon", FAR)
    near = lax.ppermute(jnp.where(core == 1, columns[0], columns[-1]), "lon", CORES)
    return far, near


def frame_halos(wide):
    up = [(i, i + 1) for i in range(FRAMES_AXIS - 1)]
    down = [(i + 1, i) for i in range(FRAMES_AXIS - 1)]
    earlier = lax.ppermute(wide[:, -1:], "frame", up)
    later = lax.ppermute(wide[:, :1], "frame", down)
    return earlier, later


VMEM = pl.BlockSpec(memory_space=pltpu.VMEM)
SMEM = pl.BlockSpec(memory_space=pltpu.SMEM)
ANY = pl.BlockSpec(memory_space=pl.ANY)


def params(mebibytes):
    return pltpu.CompilerParams(vmem_limit_bytes=mebibytes * 2**20)


def order_kernel(order_ref, kernel_ref, out_ref):
    channels = order_ref.shape[0]
    for k in range(3):
        part = slice(k * channels, (k + 1) * channels)
        moved = jnp.dot(order_ref[...], kernel_ref[part], preferred_element_type=jnp.float32)
        out_ref[part] = moved.astype(jnp.bfloat16)


def shift_rows(planes_ref, taps_ref, lat_rows):
    planes, rows, channels = planes_ref.shape
    row = lax.rem(lax.broadcasted_iota(jnp.int32, (rows, channels), 0), lat_rows)

    def plane(p, carry):
        here = planes_ref[p]
        wider = here.astype(jnp.float32)
        above = jnp.where(row == 0, 0.0, pltpu.roll(wider, 1, 0))
        below = jnp.where(row == lat_rows - 1, 0.0, pltpu.roll(wider, rows - 1, 0))
        taps_ref[0, p] = above.astype(jnp.bfloat16)
        taps_ref[1, p] = here
        taps_ref[2, p] = below.astype(jnp.bfloat16)
        return carry

    lax.fori_loop(0, planes, plane, 0)


def silu(v):
    return v * jax.nn.sigmoid(v)


def block_kernel(
    lat_rows, flags_ref, planes_any, w0, w1, w2, w3, w4, w5, w6, w7, kernel_any, bias_ref, tbias_ref,
    out_ref, planes_ref, weights_ref, kernel_ref, taps_ref, sems,
):
    pieces = (w0, w1, w2, w3, w4, w5, w6, w7)
    count = weights_ref.shape[0] // len(pieces)
    pairs = [(planes_any, planes_ref)]
    pairs += [(w, weights_ref.at[pl.ds(i * count, count)]) for i, w in enumerate(pieces)]
    pairs += [(kernel_any, kernel_ref)]
    moves = [
        pltpu.make_async_copy(source, target, sems.at[i])
        for i, (source, target) in enumerate(pairs)
    ]
    for move in moves:
        move.start()
    moves[0].wait()
    shift_rows(planes_ref, taps_ref, lat_rows)
    for move in moves[1:-1]:
        move.wait()

    planes, rows, channels = planes_ref.shape
    columns, inner = planes - 2, rows - 2 * lat_rows
    total = None
    for a in range(3):
        taps = [taps_ref[a, b : b + columns].reshape(columns * rows, channels) for b in range(3)]
        term = lax.dot_general(
            jnp.concatenate(taps, axis=1),
            weights_ref[:, 3 * a * channels : 3 * (a + 1) * channels],
            (((1,), (1,)), ((), ())),
            preferred_element_type=jnp.float32,
        )
        total = term if total is None else total + term
    active = silu(total + bias_ref[...])
    row = lax.rem(lax.broadcasted_iota(jnp.int32, active.shape, 0), rows)
    outside = (row < lat_rows) & (flags_ref[0] == 1)
    outside = outside | ((row >= rows - lat_rows) & (flags_ref[1] == 1))
    hidden = jnp.where(outside, 0.0, active).astype(jnp.bfloat16).reshape(columns, rows, channels)
    stacked = [
        hidden[:, k * lat_rows : k * lat_rows + inner].reshape(columns * inner, channels)
        for k in range(3)
    ]
    moves[-1].wait()
    mixed = jnp.dot(
        jnp.concatenate(stacked, axis=1), kernel_ref[...], preferred_element_type=jnp.float32
    )
    mixed = silu(mixed + tbias_ref[...]).reshape(columns, inner, channels)
    here = planes_ref[1 : planes - 1, lat_rows : lat_rows + inner].astype(jnp.float32)
    out_ref[...] = (here + mixed).astype(jnp.bfloat16)


def block(flags, planes, weights, kernel, bias, tbias, lat_rows):
    count, rows, channels = planes.shape
    inner = rows - 2 * lat_rows
    moved = (planes, *weights, kernel)
    joined = (len(weights) * weights[0].shape[0], weights[0].shape[1])
    shapes = (planes.shape, joined, kernel.shape, (3, *planes.shape))
    flops = (count - 2) * 2 * channels * channels * (9 * rows + 3 * inner)
    return pl.pallas_call(
        functools.partial(block_kernel, lat_rows),
        out_shape=jax.ShapeDtypeStruct((count - 2, inner, channels), jnp.bfloat16),
        in_specs=[SMEM] + [ANY] * len(moved) + [VMEM, VMEM],
        out_specs=VMEM,
        scratch_shapes=[pltpu.VMEM(s, jnp.bfloat16) for s in shapes]
        + [pltpu.SemaphoreType.DMA((len(moved),))],
        compiler_params=params(34),
        cost_estimate=pl.CostEstimate(flops=flops, bytes_accessed=2**24, transcendentals=0),
    )(flags, *moved, bias, tbias)


def reordered(order, kernel):
    return pl.pallas_call(
        order_kernel,
        out_shape=jax.ShapeDtypeStruct(kernel.shape, jnp.bfloat16),
        in_specs=[VMEM, VMEM],
        out_specs=VMEM,
        compiler_params=params(16),
        cost_estimate=pl.CostEstimate(
            flops=2 * 10**10, bytes_accessed=2**23, transcendentals=0
        ),
    )(order, kernel)


def body(latents, spatial_kernel, spatial_bias, temporal_kernel, temporal_bias):
    frames, lat_rows, lon_cols, channels = latents.shape
    core = lax.axis_index("lon") % 2
    columns = latents.transpose(2, 0, 1, 3)
    far, near = lon_halos(columns)
    along_z = gather_z(spatial_kernel)
    _, temporal_kernel = lax.optimization_barrier((along_z, temporal_kernel))
    order = channel_order()[:, None] == lax.broadcasted_iota(jnp.int32, (channels, channels), 1)
    bias = jnp.sum(jnp.where(order, spatial_bias[None, :], 0.0), axis=1)
    ordered = [
        jnp.dot(order.astype(jnp.bfloat16), temporal_kernel[k * channels : (k + 1) * channels])
        for k in range(3)
    ]
    ordered = jnp.concatenate(ordered, axis=0)
    mine = joined_x(over_x(along_z))
    pieces = over_y(mine)
    others = [lax.ppermute(mine, "lon", CORES)]
    far, near, columns, _ = lax.optimization_barrier((far, near, columns, mine))
    before = jnp.where(core == 1, near, far)
    after = jnp.where(core == 1, far, near)
    wide = jnp.concatenate([before[None], columns, after[None]], axis=0)
    earlier, later = frame_halos(wide)
    earlier, later, ordered, pieces[-1] = lax.optimization_barrier(
        (earlier, later, ordered, pieces[-1])
    )
    others += [lax.ppermute(piece, "lon", CORES) for piece in pieces[1:]]
    weights = [piece for pair in zip(pieces, others) for piece in pair]
    planes = jnp.concatenate([earlier, wide, later], axis=1)
    planes = planes.reshape(lon_cols + 2, (frames + 2) * lat_rows, channels)

    frame = lax.axis_index("frame")
    flags = jnp.stack([frame == 0, frame == FRAMES_AXIS - 1]).astype(jnp.int32)
    result = block(
        flags, planes, weights, ordered, bias[None], temporal_bias[None], lat_rows
    )
    return result.reshape(lon_cols, frames, lat_rows, channels).transpose(1, 2, 0, 3)


def solution(mesh):
    placed = (P("frame", None, "lon", None), P("frame", "lon"), P(), P(), P())
    return jax.shard_map(
        body, mesh=mesh, in_specs=placed, out_specs=P("frame", None, "lon", None), check_vma=False
    )
```

```python
import functools

import jax
import jax.numpy as jnp
import numpy as np
from jax import lax
from jax.experimental import pallas as pl
from jax.experimental.pallas import tpu as pltpu
from jax.sharding import PartitionSpec as P

LONS = 16
FRAMES_AXIS = 32
Y = 4
X = 4
Z_LO = 8


def lon_index(y, z_hi, core):
    return y * 4 + z_hi * 2 + core


def frame_index(x, z_lo):
    return x * Z_LO + z_lo


def z_groups():
    return [
        [
            lon_index(y, z_hi, core) * FRAMES_AXIS + frame_index(x, z_lo)
            for z_hi in range(2)
            for z_lo in range(Z_LO)
        ]
        for x in range(X)
        for y in range(Y)
        for core in range(2)
    ]


def x_groups():
    return [[frame_index(x, z_lo) for x in range(X)] for z_lo in range(Z_LO)]


def across_y(k):
    return [((y ^ k) * 4 + r, y * 4 + r) for y in range(Y) for r in range(4)]


NEAR_FIRST = (0, 2, 1, 3)
CORES = [(i, i ^ 1) for i in range(LONS)]
FAR = [(i, (i + 1) % LONS if i % 2 else (i - 1) % LONS) for i in range(LONS)]


def copies(piece, count):
    return jnp.broadcast_to(piece[None], (count,) + piece.shape)


def gather_z(spatial_kernel):
    shard = spatial_kernel.T
    cols, rows = shard.shape
    along_z = lax.all_to_all(
        copies(shard, 16), ("lon", "frame"), 0, 0, axis_index_groups=z_groups()
    )
    along_z = along_z.reshape(2, Z_LO, cols, rows).transpose(0, 2, 1, 3)
    return along_z.reshape(2 * cols, Z_LO * rows)


def over_x(block):
    return lax.all_to_all(copies(block, X), "frame", 0, 0, axis_index_groups=x_groups())


def over_y(block):
    return [block] + [lax.ppermute(block, "lon", across_y(k)) for k in NEAR_FIRST[1:]]


def joined_x(along_x):
    return jnp.concatenate([along_x[x] for x in range(X)], axis=1)


def channel_order():
    lon = lax.axis_index("lon")
    blocks = [(k, side, z_hi) for k in NEAR_FIRST for side in range(2) for z_hi in range(2)]
    row, side, z_hi = (jnp.asarray(np.repeat(np.array(v), 40)) for v in zip(*blocks))
    within = jnp.asarray(np.tile(np.arange(40), LONS))
    return lon_index((lon // 4) ^ row, z_hi, (lon % 2) ^ side) * 40 + within


def lon_halos(columns):
    core = lax.axis_index("lon") % 2
    far = lax.ppermute(jnp.where(core == 1, columns[-1], columns[0]), "lon", FAR)
    near = lax.ppermute(jnp.where(core == 1, columns[0], columns[-1]), "lon", CORES)
    return far, near


def frame_halos(wide):
    up = [(i, i + 1) for i in range(FRAMES_AXIS - 1)]
    down = [(i + 1, i) for i in range(FRAMES_AXIS - 1)]
    earlier = lax.ppermute(wide[:, -1:], "frame", up)
    later = lax.ppermute(wide[:, :1], "frame", down)
    return earlier, later


VMEM = pl.BlockSpec(memory_space=pltpu.VMEM)
SMEM = pl.BlockSpec(memory_space=pltpu.SMEM)
ANY = pl.BlockSpec(memory_space=pl.ANY)


def params(mebibytes):
    return pltpu.CompilerParams(vmem_limit_bytes=mebibytes * 2**20)


def shift_rows(planes_ref, taps_ref, lat_rows):
    planes, rows, channels = planes_ref.shape
    row = lax.rem(lax.broadcasted_iota(jnp.int32, (rows, channels), 0), lat_rows)

    def plane(p, carry):
        here = planes_ref[p]
        wider = here.astype(jnp.float32)
        above = jnp.where(row == 0, 0.0, pltpu.roll(wider, 1, 0))
        below = jnp.where(row == lat_rows - 1, 0.0, pltpu.roll(wider, rows - 1, 0))
        taps_ref[0, p] = above.astype(jnp.bfloat16)
        taps_ref[1, p] = here
        taps_ref[2, p] = below.astype(jnp.bfloat16)
        return carry

    lax.fori_loop(0, planes, plane, 0)


def silu(v):
    return v * jax.nn.sigmoid(v)


def block_kernel(
    lat_rows, flags_ref, planes_any, w0, w1, w2, w3, w4, w5, w6, w7, kernel_any, bias_ref, tbias_ref,
    out_ref, planes_ref, weights_ref, kernel_ref, taps_ref, sems,
):
    pieces = (w0, w1, w2, w3, w4, w5, w6, w7)
    count = weights_ref.shape[0] // len(pieces)
    third = weights_ref.shape[1] // 3
    pairs = [(planes_any, planes_ref)]
    pairs += [
        (
            w.at[:, pl.ds(a * third, third)],
            weights_ref.at[pl.ds(i * count, count), pl.ds(a * third, third)],
        )
        for a in range(3)
        for i, w in enumerate(pieces)
    ]
    pairs += [(kernel_any, kernel_ref)]
    moves = [
        pltpu.make_async_copy(source, target, sems.at[i])
        for i, (source, target) in enumerate(pairs)
    ]
    for move in moves:
        move.start()
    moves[0].wait()
    shift_rows(planes_ref, taps_ref, lat_rows)

    planes, rows, channels = planes_ref.shape
    columns, inner = planes - 2, rows - 2 * lat_rows
    total = None
    for a in range(3):
        for move in moves[1 + a * len(pieces) : 1 + (a + 1) * len(pieces)]:
            move.wait()
        taps = [taps_ref[a, b : b + columns].reshape(columns * rows, channels) for b in range(3)]
        term = lax.dot_general(
            jnp.concatenate(taps, axis=1),
            weights_ref[:, 3 * a * channels : 3 * (a + 1) * channels],
            (((1,), (1,)), ((), ())),
            preferred_element_type=jnp.float32,
        )
        total = term if total is None else total + term
    active = silu(total + bias_ref[...])
    row = lax.rem(lax.broadcasted_iota(jnp.int32, active.shape, 0), rows)
    outside = (row < lat_rows) & (flags_ref[0] == 1)
    outside = outside | ((row >= rows - lat_rows) & (flags_ref[1] == 1))
    hidden = jnp.where(outside, 0.0, active).astype(jnp.bfloat16).reshape(columns, rows, channels)
    stacked = [
        hidden[:, k * lat_rows : k * lat_rows + inner].reshape(columns * inner, channels)
        for k in range(3)
    ]
    moves[-1].wait()
    mixed = jnp.dot(
        jnp.concatenate(stacked, axis=1), kernel_ref[...], preferred_element_type=jnp.float32
    )
    mixed = silu(mixed + tbias_ref[...]).reshape(columns, inner, channels)
    here = planes_ref[1 : planes - 1, lat_rows : lat_rows + inner].astype(jnp.float32)
    out_ref[...] = (here + mixed).astype(jnp.bfloat16)


def block(flags, planes, weights, kernel, bias, tbias, lat_rows):
    count, rows, channels = planes.shape
    inner = rows - 2 * lat_rows
    moved = (planes, *weights, kernel)
    joined = (len(weights) * weights[0].shape[0], weights[0].shape[1])
    shapes = (planes.shape, joined, kernel.shape, (3, *planes.shape))
    flops = (count - 2) * 2 * channels * channels * (9 * rows + 3 * inner)
    return pl.pallas_call(
        functools.partial(block_kernel, lat_rows),
        out_shape=jax.ShapeDtypeStruct((count - 2, inner, channels), jnp.bfloat16),
        in_specs=[SMEM] + [ANY] * len(moved) + [VMEM, VMEM],
        out_specs=VMEM,
        scratch_shapes=[pltpu.VMEM(s, jnp.bfloat16) for s in shapes]
        + [pltpu.SemaphoreType.DMA((3 * len(weights) + 2,))],
        compiler_params=params(34),
        cost_estimate=pl.CostEstimate(flops=flops, bytes_accessed=2**24, transcendentals=0),
    )(flags, *moved, bias, tbias)


def body(latents, spatial_kernel, spatial_bias, temporal_kernel, temporal_bias):
    frames, lat_rows, lon_cols, channels = latents.shape
    core = lax.axis_index("lon") % 2
    columns = latents.transpose(2, 0, 1, 3)
    far, near = lon_halos(columns)
    along_z = gather_z(spatial_kernel)
    _, temporal_kernel = lax.optimization_barrier((along_z, temporal_kernel))
    order = channel_order()[:, None] == lax.broadcasted_iota(jnp.int32, (channels, channels), 1)
    bias = jnp.sum(jnp.where(order, spatial_bias[None, :], 0.0), axis=1)
    ordered = [
        jnp.dot(order.astype(jnp.bfloat16), temporal_kernel[k * channels : (k + 1) * channels])
        for k in range(3)
    ]
    ordered = jnp.concatenate(ordered, axis=0)
    mine = joined_x(over_x(along_z))
    pieces = over_y(mine)
    others = [lax.ppermute(mine, "lon", CORES)]
    far, near, columns, _ = lax.optimization_barrier((far, near, columns, mine))
    before = jnp.where(core == 1, near, far)
    after = jnp.where(core == 1, far, near)
    wide = jnp.concatenate([before[None], columns, after[None]], axis=0)
    earlier, later = frame_halos(wide)
    planes = jnp.concatenate([earlier, wide, later], axis=1)
    planes, ordered, pieces[3] = lax.optimization_barrier((planes, ordered, pieces[3]))
    others += [lax.ppermute(piece, "lon", CORES) for piece in pieces[1:]]
    weights = [piece for pair in zip(pieces, others) for piece in pair]
    planes = planes.reshape(lon_cols + 2, (frames + 2) * lat_rows, channels)

    frame = lax.axis_index("frame")
    flags = jnp.stack([frame == 0, frame == FRAMES_AXIS - 1]).astype(jnp.int32)
    result = block(
        flags, planes, weights, ordered, bias[None], temporal_bias[None], lat_rows
    )
    return result.reshape(lon_cols, frames, lat_rows, channels).transpose(1, 2, 0, 3)


def solution(mesh):
    placed = (P("frame", None, "lon", None), P("frame", "lon"), P(), P(), P())
    return jax.shard_map(
        body, mesh=mesh, in_specs=placed, out_specs=P("frame", None, "lon", None), check_vma=False
    )
```

```python
import functools

import jax
import jax.numpy as jnp
import numpy as np
from jax import lax
from jax.experimental import pallas as pl
from jax.experimental.pallas import tpu as pltpu
from jax.sharding import PartitionSpec as P

LONS = 16
FRAMES_AXIS = 32
Y = 4
X = 4
Z_LO = 8


def lon_index(y, z_hi, core):
    return y * 4 + z_hi * 2 + core


def frame_index(x, z_lo):
    return x * Z_LO + z_lo


def z_groups():
    return [
        [
            lon_index(y, z_hi, core) * FRAMES_AXIS + frame_index(x, z_lo)
            for z_hi in range(2)
            for z_lo in range(Z_LO)
        ]
        for x in range(X)
        for y in range(Y)
        for core in range(2)
    ]


def x_groups():
    return [[frame_index(x, z_lo) for x in range(X)] for z_lo in range(Z_LO)]


def across_y(k):
    return [((y ^ k) * 4 + r, y * 4 + r) for y in range(Y) for r in range(4)]


NEAR_FIRST = (0, 1, 3, 2)
CORES = [(i, i ^ 1) for i in range(LONS)]
FAR = [(i, (i + 1) % LONS if i % 2 else (i - 1) % LONS) for i in range(LONS)]


def copies(piece, count):
    return jnp.broadcast_to(piece[None], (count,) + piece.shape)


def gather_z(spatial_kernel):
    shard = spatial_kernel.T
    cols, rows = shard.shape
    along_z = lax.all_to_all(
        copies(shard, 16), ("lon", "frame"), 0, 0, axis_index_groups=z_groups()
    )
    along_z = along_z.reshape(2, Z_LO, cols, rows).transpose(0, 2, 1, 3)
    return along_z.reshape(2 * cols, Z_LO * rows)


def over_x(block):
    return lax.all_to_all(copies(block, X), "frame", 0, 0, axis_index_groups=x_groups())


def over_y(block):
    return [block] + [lax.ppermute(block, "lon", across_y(k)) for k in NEAR_FIRST[1:]]


def joined_x(along_x):
    return jnp.concatenate([along_x[x] for x in range(X)], axis=1)


def channel_order():
    lon = lax.axis_index("lon")
    blocks = [(k, side, z_hi) for k in NEAR_FIRST for side in range(2) for z_hi in range(2)]
    row, side, z_hi = (jnp.asarray(np.repeat(np.array(v), 40)) for v in zip(*blocks))
    within = jnp.asarray(np.tile(np.arange(40), LONS))
    return lon_index((lon // 4) ^ row, z_hi, (lon % 2) ^ side) * 40 + within


def lon_halos(columns):
    core = lax.axis_index("lon") % 2
    far = lax.ppermute(jnp.where(core == 1, columns[-1], columns[0]), "lon", FAR)
    near = lax.ppermute(jnp.where(core == 1, columns[0], columns[-1]), "lon", CORES)
    return far, near


def frame_halos(wide):
    up = [(i, i + 1) for i in range(FRAMES_AXIS - 1)]
    down = [(i + 1, i) for i in range(FRAMES_AXIS - 1)]
    earlier = lax.ppermute(wide[:, -1:], "frame", up)
    later = lax.ppermute(wide[:, :1], "frame", down)
    return earlier, later


VMEM = pl.BlockSpec(memory_space=pltpu.VMEM)
SMEM = pl.BlockSpec(memory_space=pltpu.SMEM)
ANY = pl.BlockSpec(memory_space=pl.ANY)


def params(mebibytes):
    return pltpu.CompilerParams(vmem_limit_bytes=mebibytes * 2**20)


def shift_rows(planes_ref, taps_ref, lat_rows):
    planes, rows, channels = planes_ref.shape
    row = lax.rem(lax.broadcasted_iota(jnp.int32, (rows, channels), 0), lat_rows)

    def plane(p, carry):
        here = planes_ref[p]
        wider = here.astype(jnp.float32)
        above = jnp.where(row == 0, 0.0, pltpu.roll(wider, 1, 0))
        below = jnp.where(row == lat_rows - 1, 0.0, pltpu.roll(wider, rows - 1, 0))
        taps_ref[0, p] = above.astype(jnp.bfloat16)
        taps_ref[1, p] = here
        taps_ref[2, p] = below.astype(jnp.bfloat16)
        return carry

    lax.fori_loop(0, planes, plane, 0)


def silu(v):
    return v * jax.nn.sigmoid(v)


def block_kernel(
    lat_rows, flags_ref, wide_any, earlier_any, later_any, w0, w1, w2, w3, w4, w5, w6, w7, kernel_any,
    bias_ref, tbias_ref, out_ref, planes_ref, weights_ref, kernel_ref, taps_ref, sems,
):
    pieces = (w0, w1, w2, w3, w4, w5, w6, w7)
    count = weights_ref.shape[0] // len(pieces)
    third = weights_ref.shape[1] // 3
    held = planes_ref.shape[1]
    pairs = [
        (wide_any, planes_ref.at[:, pl.ds(lat_rows, held - 2 * lat_rows)]),
        (earlier_any, planes_ref.at[:, pl.ds(0, lat_rows)]),
        (later_any, planes_ref.at[:, pl.ds(held - lat_rows, lat_rows)]),
    ]
    pairs += [
        (
            w.at[:, pl.ds(a * third, third)],
            weights_ref.at[pl.ds(i * count, count), pl.ds(a * third, third)],
        )
        for a in range(3)
        for i, w in enumerate(pieces)
    ]
    pairs += [(kernel_any, kernel_ref)]
    moves = [
        pltpu.make_async_copy(source, target, sems.at[i])
        for i, (source, target) in enumerate(pairs)
    ]
    for move in moves:
        move.start()
    for move in moves[:3]:
        move.wait()
    shift_rows(planes_ref, taps_ref, lat_rows)

    planes, rows, channels = planes_ref.shape
    columns, inner = planes - 2, rows - 2 * lat_rows
    total = None
    for a in range(3):
        for move in moves[3 + a * len(pieces) : 3 + (a + 1) * len(pieces)]:
            move.wait()
        taps = [taps_ref[a, b : b + columns].reshape(columns * rows, channels) for b in range(3)]
        term = lax.dot_general(
            jnp.concatenate(taps, axis=1),
            weights_ref[:, 3 * a * channels : 3 * (a + 1) * channels],
            (((1,), (1,)), ((), ())),
            preferred_element_type=jnp.float32,
        )
        total = term if total is None else total + term
    active = silu(total + bias_ref[...])
    row = lax.rem(lax.broadcasted_iota(jnp.int32, active.shape, 0), rows)
    outside = (row < lat_rows) & (flags_ref[0] == 1)
    outside = outside | ((row >= rows - lat_rows) & (flags_ref[1] == 1))
    hidden = jnp.where(outside, 0.0, active).astype(jnp.bfloat16).reshape(columns, rows, channels)
    stacked = [
        hidden[:, k * lat_rows : k * lat_rows + inner].reshape(columns * inner, channels)
        for k in range(3)
    ]
    moves[-1].wait()
    mixed = jnp.dot(
        jnp.concatenate(stacked, axis=1), kernel_ref[...], preferred_element_type=jnp.float32
    )
    mixed = silu(mixed + tbias_ref[...]).reshape(columns, inner, channels)
    here = planes_ref[1 : planes - 1, lat_rows : lat_rows + inner].astype(jnp.float32)
    out_ref[...] = (here + mixed).astype(jnp.bfloat16)


def block(flags, wide, earlier, later, weights, kernel, bias, tbias, lat_rows):
    count, inner, channels = wide.shape
    rows = inner + 2 * lat_rows
    planes = jax.ShapeDtypeStruct((count, rows, channels), wide.dtype)
    moved = (wide, earlier, later, *weights, kernel)
    joined = (len(weights) * weights[0].shape[0], weights[0].shape[1])
    shapes = (planes.shape, joined, kernel.shape, (3, *planes.shape))
    flops = (count - 2) * 2 * channels * channels * (9 * rows + 3 * inner)
    return pl.pallas_call(
        functools.partial(block_kernel, lat_rows),
        out_shape=jax.ShapeDtypeStruct((count - 2, inner, channels), jnp.bfloat16),
        in_specs=[SMEM] + [ANY] * len(moved) + [VMEM, VMEM],
        out_specs=VMEM,
        scratch_shapes=[pltpu.VMEM(s, jnp.bfloat16) for s in shapes]
        + [pltpu.SemaphoreType.DMA((3 * len(weights) + 4,))],
        compiler_params=params(34),
        cost_estimate=pl.CostEstimate(flops=flops, bytes_accessed=2**24, transcendentals=0),
    )(flags, *moved, bias, tbias)


def body(latents, spatial_kernel, spatial_bias, temporal_kernel, temporal_bias):
    frames, lat_rows, lon_cols, channels = latents.shape
    core = lax.axis_index("lon") % 2
    columns = latents.transpose(2, 0, 1, 3)
    far, near = lon_halos(columns)
    along_z = gather_z(spatial_kernel)
    _, temporal_kernel = lax.optimization_barrier((along_z, temporal_kernel))
    order = channel_order()[:, None] == lax.broadcasted_iota(jnp.int32, (channels, channels), 1)
    bias = jnp.sum(jnp.where(order, spatial_bias[None, :], 0.0), axis=1)
    ordered = [
        jnp.dot(order.astype(jnp.bfloat16), temporal_kernel[k * channels : (k + 1) * channels])
        for k in range(3)
    ]
    ordered = jnp.concatenate(ordered, axis=0)
    mine = joined_x(over_x(along_z))
    pieces = over_y(mine)
    others = [lax.ppermute(mine, "lon", CORES)]
    far, near, columns, ordered, _ = lax.optimization_barrier((far, near, columns, ordered, mine))
    before = jnp.where(core == 1, near, far)
    after = jnp.where(core == 1, far, near)
    wide = jnp.concatenate([before[None], columns, after[None]], axis=0)
    earlier, later = frame_halos(wide)
    earlier, later, pieces[3] = lax.optimization_barrier((earlier, later, pieces[3]))
    others += [lax.ppermute(piece, "lon", CORES) for piece in pieces[1:]]
    weights = [piece for pair in zip(pieces, others) for piece in pair]

    frame = lax.axis_index("frame")
    flags = jnp.stack([frame == 0, frame == FRAMES_AXIS - 1]).astype(jnp.int32)
    result = block(
        flags,
        wide.reshape(lon_cols + 2, frames * lat_rows, channels),
        earlier.reshape(lon_cols + 2, lat_rows, channels),
        later.reshape(lon_cols + 2, lat_rows, channels),
        weights,
        ordered,
        bias[None],
        temporal_bias[None],
        lat_rows,
    )
    return result.reshape(lon_cols, frames, lat_rows, channels).transpose(1, 2, 0, 3)


def solution(mesh):
    placed = (P("frame", None, "lon", None), P("frame", "lon"), P(), P(), P())
    return jax.shard_map(
        body, mesh=mesh, in_specs=placed, out_specs=P("frame", None, "lon", None), check_vma=False
    )
```

```python
import functools

import jax
import jax.numpy as jnp
import numpy as np
from jax import lax
from jax.experimental import pallas as pl
from jax.experimental.pallas import tpu as pltpu
from jax.sharding import PartitionSpec as P

LONS = 16
FRAMES_AXIS = 32
Y = 4
X = 4
Z_LO = 8


def lon_index(y, z_hi, core):
    return y * 4 + z_hi * 2 + core


def frame_index(x, z_lo):
    return x * Z_LO + z_lo


def z_groups():
    return [
        [
            lon_index(y, z_hi, core) * FRAMES_AXIS + frame_index(x, z_lo)
            for z_hi in range(2)
            for z_lo in range(Z_LO)
        ]
        for x in range(X)
        for y in range(Y)
        for core in range(2)
    ]


def x_groups():
    return [[frame_index(x, z_lo) for x in range(X)] for z_lo in range(Z_LO)]


def across_y(k):
    return [((y ^ k) * 4 + r, y * 4 + r) for y in range(Y) for r in range(4)]


NEAR_FIRST = (0, 1, 3, 2)
CORES = [(i, i ^ 1) for i in range(LONS)]
FAR = [(i, (i + 1) % LONS if i % 2 else (i - 1) % LONS) for i in range(LONS)]


def copies(piece, count):
    return jnp.broadcast_to(piece[None], (count,) + piece.shape)


def gather_z(spatial_kernel):
    shard = spatial_kernel.T
    cols, rows = shard.shape
    along_z = lax.all_to_all(
        copies(shard, 16), ("lon", "frame"), 0, 0, axis_index_groups=z_groups()
    )
    along_z = along_z.reshape(2, Z_LO, cols, rows).transpose(0, 2, 1, 3)
    return along_z.reshape(2 * cols, Z_LO * rows)


def over_x(block):
    return lax.all_to_all(copies(block, X), "frame", 0, 0, axis_index_groups=x_groups())


def over_y(block):
    return [block] + [lax.ppermute(block, "lon", across_y(k)) for k in NEAR_FIRST[1:]]


def joined_x(along_x):
    return jnp.concatenate([along_x[x] for x in range(X)], axis=1)


def channel_order():
    lon = lax.axis_index("lon")
    blocks = [(k, side, z_hi) for k in NEAR_FIRST for side in range(2) for z_hi in range(2)]
    row, side, z_hi = (jnp.asarray(np.repeat(np.array(v), 40)) for v in zip(*blocks))
    within = jnp.asarray(np.tile(np.arange(40), LONS))
    return lon_index((lon // 4) ^ row, z_hi, (lon % 2) ^ side) * 40 + within


def lon_halos(columns):
    core = lax.axis_index("lon") % 2
    far = lax.ppermute(jnp.where(core == 1, columns[-1], columns[0]), "lon", FAR)
    near = lax.ppermute(jnp.where(core == 1, columns[0], columns[-1]), "lon", CORES)
    return far, near


def frame_halos(wide):
    up = [(i, i + 1) for i in range(FRAMES_AXIS - 1)]
    down = [(i + 1, i) for i in range(FRAMES_AXIS - 1)]
    earlier = lax.ppermute(wide[:, -1:], "frame", up)
    later = lax.ppermute(wide[:, :1], "frame", down)
    return earlier, later


VMEM = pl.BlockSpec(memory_space=pltpu.VMEM)
SMEM = pl.BlockSpec(memory_space=pltpu.SMEM)
ANY = pl.BlockSpec(memory_space=pl.ANY)


def params(mebibytes):
    return pltpu.CompilerParams(vmem_limit_bytes=mebibytes * 2**20)


def shift_rows(planes_ref, taps_ref, lat_rows):
    planes, rows, channels = planes_ref.shape
    row = lax.rem(lax.broadcasted_iota(jnp.int32, (rows, channels), 0), lat_rows)

    def plane(p, carry):
        here = planes_ref[p]
        wider = here.astype(jnp.float32)
        above = jnp.where(row == 0, 0.0, pltpu.roll(wider, 1, 0))
        below = jnp.where(row == lat_rows - 1, 0.0, pltpu.roll(wider, rows - 1, 0))
        taps_ref[0, p] = above.astype(jnp.bfloat16)
        taps_ref[1, p] = here
        taps_ref[2, p] = below.astype(jnp.bfloat16)
        return carry

    lax.fori_loop(0, planes, plane, 0)


def silu(v):
    return v * jax.nn.sigmoid(v)


def block_kernel(
    lat_rows, flags_ref, wide_any, earlier_any, later_any, w0, w1, w2, w3, w4, w5, w6, w7, t0, t1, t2,
    bias_ref, tbias_ref, out_ref, planes_ref, weights_ref, kernel_ref, taps_ref, sems,
):
    pieces = (w0, w1, w2, w3, w4, w5, w6, w7)
    count = weights_ref.shape[0] // len(pieces)
    third = weights_ref.shape[1] // 3
    held = planes_ref.shape[1]
    pairs = [
        (wide_any, planes_ref.at[:, pl.ds(lat_rows, held - 2 * lat_rows)]),
        (earlier_any, planes_ref.at[:, pl.ds(0, lat_rows)]),
        (later_any, planes_ref.at[:, pl.ds(held - lat_rows, lat_rows)]),
    ]
    pairs += [
        (
            w.at[:, pl.ds(a * third, third)],
            weights_ref.at[pl.ds(i * count, count), pl.ds(a * third, third)],
        )
        for a in range(3)
        for i, w in enumerate(pieces)
    ]
    channels = planes_ref.shape[2]
    pairs += [
        (t, kernel_ref.at[pl.ds(k * channels, channels)]) for k, t in enumerate((t0, t1, t2))
    ]
    moves = [
        pltpu.make_async_copy(source, target, sems.at[i])
        for i, (source, target) in enumerate(pairs)
    ]
    for move in moves:
        move.start()
    for move in moves[:3]:
        move.wait()
    shift_rows(planes_ref, taps_ref, lat_rows)

    planes, rows, channels = planes_ref.shape
    columns, inner = planes - 2, rows - 2 * lat_rows
    total = None
    for first, end in ((0, 1), (1, 3)):
        for move in moves[3 + first * len(pieces) : 3 + end * len(pieces)]:
            move.wait()
        taps = [
            taps_ref[a, b : b + columns].reshape(columns * rows, channels)
            for a in range(first, end)
            for b in range(3)
        ]
        term = lax.dot_general(
            jnp.concatenate(taps, axis=1),
            weights_ref[:, 3 * first * channels : 3 * end * channels],
            (((1,), (1,)), ((), ())),
            preferred_element_type=jnp.float32,
        )
        total = term if total is None else total + term
    active = silu(total + bias_ref[...])
    row = lax.rem(lax.broadcasted_iota(jnp.int32, active.shape, 0), rows)
    outside = (row < lat_rows) & (flags_ref[0] == 1)
    outside = outside | ((row >= rows - lat_rows) & (flags_ref[1] == 1))
    hidden = jnp.where(outside, 0.0, active).astype(jnp.bfloat16).reshape(columns, rows, channels)
    stacked = [
        hidden[:, k * lat_rows : k * lat_rows + inner].reshape(columns * inner, channels)
        for k in range(3)
    ]
    for move in moves[-3:]:
        move.wait()
    mixed = jnp.dot(
        jnp.concatenate(stacked, axis=1), kernel_ref[...], preferred_element_type=jnp.float32
    )
    mixed = silu(mixed + tbias_ref[...]).reshape(columns, inner, channels)
    here = planes_ref[1 : planes - 1, lat_rows : lat_rows + inner].astype(jnp.float32)
    out_ref[...] = (here + mixed).astype(jnp.bfloat16)


def block(flags, wide, earlier, later, weights, kernel, bias, tbias, lat_rows):
    count, inner, channels = wide.shape
    rows = inner + 2 * lat_rows
    planes = jax.ShapeDtypeStruct((count, rows, channels), wide.dtype)
    moved = (wide, earlier, later, *weights, *kernel)
    joined = (len(weights) * weights[0].shape[0], weights[0].shape[1])
    shapes = (planes.shape, joined, (3 * channels, channels), (3, *planes.shape))
    flops = (count - 2) * 2 * channels * channels * (9 * rows + 3 * inner)
    return pl.pallas_call(
        functools.partial(block_kernel, lat_rows),
        out_shape=jax.ShapeDtypeStruct((count - 2, inner, channels), jnp.bfloat16),
        in_specs=[SMEM] + [ANY] * len(moved) + [VMEM, VMEM],
        out_specs=VMEM,
        scratch_shapes=[pltpu.VMEM(s, jnp.bfloat16) for s in shapes]
        + [pltpu.SemaphoreType.DMA((3 * len(weights) + 6,))],
        compiler_params=params(34),
        cost_estimate=pl.CostEstimate(flops=flops, bytes_accessed=2**24, transcendentals=0),
    )(flags, *moved, bias, tbias)


def body(latents, spatial_kernel, spatial_bias, temporal_kernel, temporal_bias):
    frames, lat_rows, lon_cols, channels = latents.shape
    core = lax.axis_index("lon") % 2
    columns = latents.transpose(2, 0, 1, 3)
    far, near = lon_halos(columns)
    along_z = gather_z(spatial_kernel)
    _, temporal_kernel = lax.optimization_barrier((along_z, temporal_kernel))
    order = channel_order()[:, None] == lax.broadcasted_iota(jnp.int32, (channels, channels), 1)
    bias = jnp.sum(jnp.where(order, spatial_bias[None, :], 0.0), axis=1)
    ordered = [
        jnp.dot(order.astype(jnp.bfloat16), temporal_kernel[k * channels : (k + 1) * channels])
        for k in range(3)
    ]
    mine = joined_x(over_x(along_z))
    mine, *ordered = lax.optimization_barrier((mine, *ordered))
    pieces = over_y(mine)
    others = [lax.ppermute(mine, "lon", CORES)]
    far, near, columns, *ordered = lax.optimization_barrier((far, near, columns, *ordered))
    before = jnp.where(core == 1, near, far)
    after = jnp.where(core == 1, far, near)
    wide = jnp.concatenate([before[None], columns, after[None]], axis=0)
    earlier, later = frame_halos(wide)
    earlier, later, pieces[3] = lax.optimization_barrier((earlier, later, pieces[3]))
    others += [lax.ppermute(piece, "lon", CORES) for piece in pieces[1:]]
    weights = [piece for pair in zip(pieces, others) for piece in pair]

    frame = lax.axis_index("frame")
    flags = jnp.stack([frame == 0, frame == FRAMES_AXIS - 1]).astype(jnp.int32)
    result = block(
        flags,
        wide.reshape(lon_cols + 2, frames * lat_rows, channels),
        earlier.reshape(lon_cols + 2, lat_rows, channels),
        later.reshape(lon_cols + 2, lat_rows, channels),
        weights,
        ordered,
        bias[None],
        temporal_bias[None],
        lat_rows,
    )
    return result.reshape(lon_cols, frames, lat_rows, channels).transpose(1, 2, 0, 3)


def solution(mesh):
    placed = (P("frame", None, "lon", None), P("frame", "lon"), P(), P(), P())
    return jax.shard_map(
        body, mesh=mesh, in_specs=placed, out_specs=P("frame", None, "lon", None), check_vma=False
    )
```

```python
import functools

import jax
import jax.numpy as jnp
import numpy as np
from jax import lax
from jax.experimental import pallas as pl
from jax.experimental.pallas import tpu as pltpu
from jax.sharding import PartitionSpec as P

LONS = 16
FRAMES_AXIS = 32
Y = 4
X = 4
Z_LO = 8


def lon_index(y, z_hi, core):
    return y * 4 + z_hi * 2 + core


def frame_index(x, z_lo):
    return x * Z_LO + z_lo


def z_groups():
    return [
        [
            lon_index(y, z_hi, core) * FRAMES_AXIS + frame_index(x, z_lo)
            for z_hi in range(2)
            for z_lo in range(Z_LO)
        ]
        for x in range(X)
        for y in range(Y)
        for core in range(2)
    ]


def x_groups():
    return [[frame_index(x, z_lo) for x in range(X)] for z_lo in range(Z_LO)]


def across_y(k):
    return [((y ^ k) * 4 + r, y * 4 + r) for y in range(Y) for r in range(4)]


NEAR_FIRST = (0, 1, 3, 2)
CORES = [(i, i ^ 1) for i in range(LONS)]
FAR = [(i, (i + 1) % LONS if i % 2 else (i - 1) % LONS) for i in range(LONS)]


def copies(piece, count):
    return jnp.broadcast_to(piece[None], (count,) + piece.shape)


def gather_z(spatial_kernel):
    shard = spatial_kernel.T
    cols, rows = shard.shape
    along_z = lax.all_to_all(
        copies(shard, 16), ("lon", "frame"), 0, 0, axis_index_groups=z_groups()
    )
    along_z = along_z.reshape(2, Z_LO, cols, rows).transpose(0, 2, 1, 3)
    return along_z.reshape(2 * cols, Z_LO * rows)


def over_x(block):
    return lax.all_to_all(copies(block, X), "frame", 0, 0, axis_index_groups=x_groups())


def over_y(block):
    return [block] + [lax.ppermute(block, "lon", across_y(k)) for k in NEAR_FIRST[1:]]


def joined_x(along_x):
    return jnp.concatenate([along_x[x] for x in range(X)], axis=1)


def channel_order():
    lon = lax.axis_index("lon")
    blocks = [(k, side, z_hi) for k in NEAR_FIRST for side in range(2) for z_hi in range(2)]
    row, side, z_hi = (jnp.asarray(np.repeat(np.array(v), 40)) for v in zip(*blocks))
    within = jnp.asarray(np.tile(np.arange(40), LONS))
    return lon_index((lon // 4) ^ row, z_hi, (lon % 2) ^ side) * 40 + within


def lon_halos(columns):
    core = lax.axis_index("lon") % 2
    far = lax.ppermute(jnp.where(core == 1, columns[-1], columns[0]), "lon", FAR)
    near = lax.ppermute(jnp.where(core == 1, columns[0], columns[-1]), "lon", CORES)
    return far, near


def frame_halos(wide):
    up = [(i, i + 1) for i in range(FRAMES_AXIS - 1)]
    down = [(i + 1, i) for i in range(FRAMES_AXIS - 1)]
    earlier = lax.ppermute(wide[:, -1:], "frame", up)
    later = lax.ppermute(wide[:, :1], "frame", down)
    return earlier, later


VMEM = pl.BlockSpec(memory_space=pltpu.VMEM)
SMEM = pl.BlockSpec(memory_space=pltpu.SMEM)
ANY = pl.BlockSpec(memory_space=pl.ANY)


def params(mebibytes):
    return pltpu.CompilerParams(vmem_limit_bytes=mebibytes * 2**20)


def shift_rows(planes_ref, taps_ref, lat_rows):
    planes, rows, channels = planes_ref.shape
    row = lax.rem(lax.broadcasted_iota(jnp.int32, (rows, channels), 0), lat_rows)

    def plane(p, carry):
        here = planes_ref[p]
        wider = here.astype(jnp.float32)
        above = jnp.where(row == 0, 0.0, pltpu.roll(wider, 1, 0))
        below = jnp.where(row == lat_rows - 1, 0.0, pltpu.roll(wider, rows - 1, 0))
        taps_ref[0, p] = above.astype(jnp.bfloat16)
        taps_ref[1, p] = here
        taps_ref[2, p] = below.astype(jnp.bfloat16)
        return carry

    lax.fori_loop(0, planes, plane, 0)


def silu(v):
    return v * jax.nn.sigmoid(v)


def block_kernel(
    lat_rows, flags_ref, wide_any, earlier_any, later_any, w0, w1, w2, w3, w4, w5, w6, w7, t0, t1, t2,
    bias_ref, tbias_ref, out_ref, planes_ref, weights_ref, kernel_ref, taps_ref, sems,
):
    pieces = (w0, w1, w2, w3, w4, w5, w6, w7)
    count = weights_ref.shape[0] // len(pieces)
    third = weights_ref.shape[1] // 3
    held = planes_ref.shape[1]
    pairs = [
        (wide_any, planes_ref.at[:, pl.ds(lat_rows, held - 2 * lat_rows)]),
        (earlier_any, planes_ref.at[:, pl.ds(0, lat_rows)]),
        (later_any, planes_ref.at[:, pl.ds(held - lat_rows, lat_rows)]),
    ]
    pairs += [
        (
            w.at[:, pl.ds(a * third, third)],
            weights_ref.at[pl.ds(i * count, count), pl.ds(a * third, third)],
        )
        for a in range(3)
        for i, w in enumerate(pieces)
    ]
    channels = planes_ref.shape[2]
    pairs += [
        (t, kernel_ref.at[pl.ds(k * channels, channels)]) for k, t in enumerate((t0, t1, t2))
    ]
    moves = [
        pltpu.make_async_copy(source, target, sems.at[i])
        for i, (source, target) in enumerate(pairs)
    ]
    for move in moves:
        move.start()
    for move in moves[:3]:
        move.wait()
    shift_rows(planes_ref, taps_ref, lat_rows)

    planes, rows, channels = planes_ref.shape
    columns, inner = planes - 2, rows - 2 * lat_rows
    total = None
    for first, end in ((0, 1), (1, 2), (2, 3)):
        for move in moves[3 + first * len(pieces) : 3 + end * len(pieces)]:
            move.wait()
        taps = [
            taps_ref[a, b : b + columns].reshape(columns * rows, channels)
            for a in range(first, end)
            for b in range(3)
        ]
        term = lax.dot_general(
            jnp.concatenate(taps, axis=1),
            weights_ref[:, 3 * first * channels : 3 * end * channels],
            (((1,), (1,)), ((), ())),
            preferred_element_type=jnp.float32,
        )
        total = term if total is None else total + term
    active = silu(total + bias_ref[...])
    row = lax.rem(lax.broadcasted_iota(jnp.int32, active.shape, 0), rows)
    outside = (row < lat_rows) & (flags_ref[0] == 1)
    outside = outside | ((row >= rows - lat_rows) & (flags_ref[1] == 1))
    hidden = jnp.where(outside, 0.0, active).astype(jnp.bfloat16).reshape(columns, rows, channels)
    stacked = [
        hidden[:, k * lat_rows : k * lat_rows + inner].reshape(columns * inner, channels)
        for k in range(3)
    ]
    for move in moves[-3:]:
        move.wait()
    mixed = jnp.dot(
        jnp.concatenate(stacked, axis=1), kernel_ref[...], preferred_element_type=jnp.float32
    )
    mixed = silu(mixed + tbias_ref[...]).reshape(columns, inner, channels)
    here = planes_ref[1 : planes - 1, lat_rows : lat_rows + inner].astype(jnp.float32)
    out_ref[...] = (here + mixed).astype(jnp.bfloat16)


def block(flags, wide, earlier, later, weights, kernel, bias, tbias, lat_rows):
    count, inner, channels = wide.shape
    rows = inner + 2 * lat_rows
    planes = jax.ShapeDtypeStruct((count, rows, channels), wide.dtype)
    moved = (wide, earlier, later, *weights, *kernel)
    joined = (len(weights) * weights[0].shape[0], weights[0].shape[1])
    shapes = (planes.shape, joined, (3 * channels, channels), (3, *planes.shape))
    flops = (count - 2) * 2 * channels * channels * (9 * rows + 3 * inner)
    return pl.pallas_call(
        functools.partial(block_kernel, lat_rows),
        out_shape=jax.ShapeDtypeStruct((count - 2, inner, channels), jnp.bfloat16),
        in_specs=[SMEM] + [ANY] * len(moved) + [VMEM, VMEM],
        out_specs=VMEM,
        scratch_shapes=[pltpu.VMEM(s, jnp.bfloat16) for s in shapes]
        + [pltpu.SemaphoreType.DMA((3 * len(weights) + 6,))],
        compiler_params=params(34),
        cost_estimate=pl.CostEstimate(flops=flops, bytes_accessed=2**24, transcendentals=0),
    )(flags, *moved, bias, tbias)


def body(latents, spatial_kernel, spatial_bias, temporal_kernel, temporal_bias):
    frames, lat_rows, lon_cols, channels = latents.shape
    core = lax.axis_index("lon") % 2
    columns = latents.transpose(2, 0, 1, 3)
    far, near = lon_halos(columns)
    along_z = gather_z(spatial_kernel)
    _, temporal_kernel = lax.optimization_barrier((along_z, temporal_kernel))
    order = channel_order()[:, None] == lax.broadcasted_iota(jnp.int32, (channels, channels), 1)
    bias = jnp.sum(jnp.where(order, spatial_bias[None, :], 0.0), axis=1)
    ordered = [
        jnp.dot(order.astype(jnp.bfloat16), temporal_kernel[k * channels : (k + 1) * channels])
        for k in range(3)
    ]
    mine = joined_x(over_x(along_z))
    mine, *ordered = lax.optimization_barrier((mine, *ordered))
    pieces = over_y(mine)
    others = [lax.ppermute(mine, "lon", CORES)]
    far, near, columns, *ordered = lax.optimization_barrier((far, near, columns, *ordered))
    before = jnp.where(core == 1, near, far)
    after = jnp.where(core == 1, far, near)
    wide = jnp.concatenate([before[None], columns, after[None]], axis=0)
    earlier, later = frame_halos(wide)
    earlier, later, pieces[3] = lax.optimization_barrier((earlier, later, pieces[3]))
    others += [lax.ppermute(piece, "lon", CORES) for piece in pieces[1:]]
    weights = [piece for pair in zip(pieces, others) for piece in pair]

    frame = lax.axis_index("frame")
    flags = jnp.stack([frame == 0, frame == FRAMES_AXIS - 1]).astype(jnp.int32)
    result = block(
        flags,
        wide.reshape(lon_cols + 2, frames * lat_rows, channels),
        earlier.reshape(lon_cols + 2, lat_rows, channels),
        later.reshape(lon_cols + 2, lat_rows, channels),
        weights,
        ordered,
        bias[None],
        temporal_bias[None],
        lat_rows,
    )
    return result.reshape(lon_cols, frames, lat_rows, channels).transpose(1, 2, 0, 3)


def solution(mesh):
    placed = (P("frame", None, "lon", None), P("frame", "lon"), P(), P(), P())
    return jax.shard_map(
        body, mesh=mesh, in_specs=placed, out_specs=P("frame", None, "lon", None), check_vma=False
    )
```
